32 devices in a mesh: ctx: 4 (over y, x), fsdp: 8 (over z, core).
Axes of the slice: x: 2, y: 2, z: 4, core: 2. Of those that a mesh axis runs over, the one named last changes fastest.
Arguments:
- tokens: bfloat16 [8, 2048, 768], P('fsdp', 'ctx'), may hold values from -6 to 6
- cotangent: bfloat16 [8, 2048, 768], P('fsdp', 'ctx'), may hold values from -8 to 8
- ln1_gain: bfloat16 [2, 768], P(None, 'fsdp'), may hold values from 0.099609375 to 1.8984375
- ln1_bias: bfloat16 [2, 768], P(None, 'fsdp'), may hold values from -3 to 3
- w_qkv: bfloat16 [2, 768, 2304], P(None, 'fsdp'), may hold values from -0.21875 to 0.21875
- q_bias: bfloat16 [2, 768], P(None, 'fsdp'), may hold values from -6 to 6
- v_bias: bfloat16 [2, 768], P(None, 'fsdp'), may hold values from -3 to 3
- w_out: bfloat16 [2, 768, 768], P(None, 'fsdp'), may hold values from -0.4375 to 0.4375
- out_bias: bfloat16 [2, 768], P(None, 'fsdp'), may hold values from -3 to 3
- ln2_gain: bfloat16 [2, 768], P(None, 'fsdp'), may hold values from 0.099609375 to 1.8984375
- ln2_bias: bfloat16 [2, 768], P(None, 'fsdp'), may hold values from -3 to 3
- w_up: bfloat16 [2, 768, 3072], P(None, 'fsdp'), may hold values from -0.21875 to 0.21875
- up_bias: bfloat16 [2, 3072], P(None, 'fsdp'), may hold values from -3 to 3
- w_down: bfloat16 [2, 3072, 768], P(None, 'fsdp'), may hold values from -0.109375 to 0.109375
- down_bias: bfloat16 [2, 768], P(None, 'fsdp'), may hold values from -3 to 3
Outputs:
- outputs: bfloat16 [8, 2048, 768], P('fsdp', 'ctx')
- grad_tokens: float32 [8, 2048, 768], P('fsdp', 'ctx')
- grad_ln1_gain: float32 [2, 768], P(None, 'fsdp')
- grad_ln1_bias: float32 [2, 768], P(None, 'fsdp')
- grad_w_qkv: float32 [2, 768, 2304], P(None, 'fsdp')
- grad_q_bias: float32 [2, 768], P(None, 'fsdp')
- grad_v_bias: float32 [2, 768], P(None, 'fsdp')
- grad_w_out: float32 [2, 768, 768], P(None, 'fsdp')
- grad_out_bias: float32 [2, 768], P(None, 'fsdp')
- grad_ln2_gain: float32 [2, 768], P(None, 'fsdp')
- grad_ln2_bias: float32 [2, 768], P(None, 'fsdp')
- grad_w_up: float32 [2, 768, 3072], P(None, 'fsdp')
- grad_up_bias: float32 [2, 3072], P(None, 'fsdp')
- grad_w_down: float32 [2, 3072, 768], P(None, 'fsdp')
- grad_down_bias: float32 [2, 768], P(None, 'fsdp')
The draws below stay inside these ranges and needn't reach their ends.
All inputs are finite; a program needn't handle non-finite values.
Results may differ from the reference program's by a relative error of at most 0.034.
Values may be sent and summed in bfloat16 or wider, within the bound.
A program may use at most 256 MiB of HBM per device.

```python
import jax
import jax.numpy as jnp
from jax import lax

D = 768
HEADS = 12
HEAD_DIM = 64
FF = 3072
LAYERS = 2
TOK_DEV = 512
SEQ_LEN = 2048
SEQS = 8


def with_spikes(drawn, rng, source, target, parts, factor):
    owner, partner = [(jnp.arange(drawn.shape[position]) // (drawn.shape[position] // parts)).reshape([-1 if axis == position else 1 for axis in range(drawn.ndim)]) for position in (source, target)]
    chosen = jax.random.permutation(rng, parts)[partner]
    strong = (owner == chosen) | (owner == (partner + parts // 2) % parts)
    return jnp.where(strong, factor * drawn, drawn)


def block_levels(key, extent, split, least, high):
    def one(dim, shards_of):
        draws = jax.random.uniform(jax.random.fold_in(jax.random.fold_in(key, 6), dim), (shards_of,), jnp.float32, least / len(split), high / len(split))
        return jnp.repeat(jnp.exp(draws), extent[dim] // shards_of).reshape((-1,) + (1,) * (len(extent) - dim - 1))

    level = one(*split[0])
    for cut in split[1:]:
        level = level * one(*cut)
    return level


def bell_draw(own_key, extent, deviation, most, cuts=(), kind=jnp.bfloat16):
    loudness = block_levels(own_key, extent, cuts, -0.22, 0.18) if cuts else 1.0
    array = jax.random.normal(own_key, extent, jnp.float32) * deviation * loudness
    return jnp.minimum(jnp.maximum(array, -most), most).astype(kind)


def bell_draw_with(own_key, extent, width, bound, pieces, heavy, kind=jnp.bfloat16):
    values = width * jax.random.normal(own_key, extent, jnp.float32)
    if pieces:
        values = values * block_levels(own_key, extent, pieces, -0.22, 0.18)
    return jnp.clip(with_spikes(values, jax.random.fold_in(own_key, 3), *heavy), -bound, bound).astype(kind)


def setup_inputs(seed: int = 0) -> dict:
    arg_keys = jax.random.split(jax.random.key(seed), 16)
    tokens = bell_draw(arg_keys[0], (SEQS, SEQ_LEN, D), 1.0, 6.0, ((0, 8), (1, 4)))
    cotangent = bell_draw_with(arg_keys[1], (SEQS, SEQ_LEN, D), 1.0, 8.0, ((0, 8), (1, 4)), (0, 2, 8, 2.0))
    ln1_gain = jnp.clip(1.0 + 0.18 * jax.random.normal(arg_keys[2], (LAYERS, D), jnp.float32), 0.099609375, 1.8984375).astype(jnp.bfloat16)
    ln1_bias = bell_draw(arg_keys[3], (LAYERS, D), 0.5, 3.0, ((1, 8),))
    w_qkv = bell_draw(arg_keys[4], (LAYERS, D, 3 * D), D ** -0.5, 0.21875, ((1, 8),))
    q_bias = bell_draw(arg_keys[5], (LAYERS, D), 1.0, 6.0, ((1, 8),))
    v_bias = bell_draw(arg_keys[6], (LAYERS, D), 0.5, 3.0, ((1, 8),))
    w_out = bell_draw(arg_keys[7], (LAYERS, D, D), (D // 4) ** -0.5, 0.4375, ((1, 8),))
    out_bias = bell_draw(arg_keys[8], (LAYERS, D), 0.5, 3.0, ((1, 8),))
    ln2_gain = jnp.clip(1.0 + 0.18 * jax.random.normal(arg_keys[9], (LAYERS, D), jnp.float32), 0.099609375, 1.8984375).astype(jnp.bfloat16)
    ln2_bias = bell_draw(arg_keys[10], (LAYERS, D), 0.5, 3.0, ((1, 8),))
    w_up = bell_draw(arg_keys[11], (LAYERS, D, FF), D ** -0.5, 0.21875, ((1, 8),))
    up_bias = bell_draw(arg_keys[12], (LAYERS, FF), 0.5, 3.0, ((1, 8),))
    w_down = bell_draw(arg_keys[13], (LAYERS, FF, D), FF ** -0.5, 0.109375, ((1, 8),))
    down_bias = bell_draw(arg_keys[14], (LAYERS, D), 0.5, 3.0, ((1, 8),))
    return {"tokens": tokens, "cotangent": cotangent, "ln1_gain": ln1_gain, "ln1_bias": ln1_bias, "w_qkv": w_qkv, "q_bias": q_bias, "v_bias": v_bias, "w_out": w_out, "out_bias": out_bias, "ln2_gain": ln2_gain, "ln2_bias": ln2_bias, "w_up": w_up, "up_bias": up_bias, "w_down": w_down, "down_bias": down_bias}


EPS = 1e-05
MASKED = -1e+30

@jax.custom_vjp
def low(v):
    return lax.optimization_barrier(v.astype(jnp.bfloat16)).astype(jnp.float32)

@jax.custom_vjp
def low_back(v):
    return v

def low_keep(v):
    return (low(v), None)

def low_pass(kept, grad):
    return (grad,)

def back_keep(v):
    return (v, None)

def back_low(kept, grad):
    return (low(grad),)
low.defvjp(low_keep, low_pass)
low_back.defvjp(back_keep, back_low)

def product(left, right):
    return jnp.dot(left, right, precision=lax.Precision.HIGHEST, preferred_element_type=jnp.float32)

def layer_norm(values, gain, shift):
    center = values - lax.optimization_barrier(jnp.mean(values, axis=-1, keepdims=True))
    spread = lax.optimization_barrier(jnp.mean(center * center, axis=-1, keepdims=True))
    return center * lax.rsqrt(spread + EPS) * gain + shift

def attention(queries, keys, values):
    length = queries.shape[0]
    key_heads = keys.reshape(length, HEADS, HEAD_DIM)
    value_heads = values.reshape(length, HEADS, HEAD_DIM)
    positions = jnp.arange(length, dtype=jnp.int32)

    def block(number):
        start = (number * TOK_DEV).astype(jnp.int32)
        query_heads = lax.dynamic_slice_in_dim(queries, start, TOK_DEV, 0).reshape(TOK_DEV, HEADS, HEAD_DIM)
        scores = low_back(jnp.einsum('qhd,khd->hqk', query_heads, key_heads, precision=lax.Precision.HIGHEST))
        query_pos = start + jnp.arange(TOK_DEV, dtype=jnp.int32)
        allowed = positions[None, :] <= query_pos[:, None]
        scores = jnp.where(allowed[None], scores, MASKED)
        highest = lax.optimization_barrier(jnp.max(scores, axis=-1, keepdims=True))
        weights = jnp.exp(scores - highest)
        probs = low(weights / lax.optimization_barrier(jnp.sum(weights, axis=-1, keepdims=True)))
        return jnp.einsum('hqk,khd->qhd', probs, value_heads, precision=lax.Precision.HIGHEST)
    blocks = lax.map(jax.checkpoint(block), jnp.arange(length // TOK_DEV, dtype=jnp.int32))
    return blocks.reshape(length, HEADS * HEAD_DIM)

def decoder_layer(inputs, params):
    gain_one, shift_one, w_qkv, q_bias, v_bias, w_out, out_bias, gain_two, shift_two, w_up, up_bias, w_down, down_bias = params
    normed = low(layer_norm(inputs, gain_one, shift_one))
    project = product(normed, w_qkv)
    queries = low(low_back((project[:, :D] + q_bias) * 0.125))
    keys = low(low_back(project[:, D:2 * D]))
    values = low(low_back(project[:, 2 * D:] + v_bias))
    attended = low(low_back(attention(queries, keys, values)))
    middle = inputs + low_back(product(attended, w_out)) + out_bias
    normed_two = low(layer_norm(middle, gain_two, shift_two))
    lifted = low_back(product(normed_two, w_up)) + up_bias
    activated = low(jax.nn.gelu(lifted, approximate=False))
    return middle + low_back(product(activated, w_down)) + down_bias

def reference(tokens, cotangent, ln1_gain, ln1_bias, w_qkv, q_bias, v_bias, w_out, out_bias, ln2_gain, ln2_bias, w_up, up_bias, w_down, down_bias):
    params = tuple((entry.astype(jnp.float32) for entry in (ln1_gain, ln1_bias, w_qkv, q_bias, v_bias, w_out, out_bias, ln2_gain, ln2_bias, w_up, up_bias, w_down, down_bias)))

    def forward(weights, inputs):
        for which_layer in range(LAYERS):
            inputs = decoder_layer(inputs, tuple((entry[which_layer] for entry in weights)))
        return inputs

    def one_sequence(totals, item):
        inputs, incoming = item
        result, back = jax.vjp(forward, params, inputs)
        grad_params, grad_inputs = back(incoming)
        totals = tuple((total + grad for total, grad in zip(totals, grad_params)))
        return (totals, (result.astype(jnp.bfloat16), grad_inputs))
    zeros = tuple((jnp.zeros_like(entry) for entry in params))
    totals, (results, grad_inputs) = lax.scan(one_sequence, zeros, (tokens.astype(jnp.float32), cotangent.astype(jnp.float32)))
    return (results, grad_inputs, totals[0], totals[1], totals[2], totals[3], totals[4], totals[5], totals[6], totals[7], totals[8], totals[9], totals[10], totals[11], totals[12])
```

```python
import functools

import jax
import jax.numpy as jnp
from jax import lax
from jax.experimental import pallas as pl
from jax.experimental.pallas import tpu as pltpu
from jax.sharding import PartitionSpec as P

HEADS = 12


EPS = 1e-05
MASKED = -1e30
MIB = 1024 * 1024


def layer_norm(values, gain, shift):
    center = values - jnp.mean(values, axis=-1, keepdims=True)
    spread = jnp.mean(center * center, axis=-1, keepdims=True)
    return center * lax.rsqrt(spread + EPS) * gain + shift


def smooth(values):
    return jax.nn.gelu(values, approximate=False)


def dot(left, right, left_dim, right_dim):
    return lax.dot_general(
        left, right, (((left_dim,), (right_dim,)), ((), ())), preferred_element_type=jnp.float32
    )


def matmul(left, right):
    return dot(left, right, 1, 0)


def matmul_left_t(left, right):
    return dot(left, right, 0, 0)


def matmul_right_t(left, right):
    return dot(left, right, 1, 1)


def causal(scores):
    key_pos = lax.broadcasted_iota(jnp.int32, scores.shape, 0)
    query_pos = lax.broadcasted_iota(jnp.int32, scores.shape, 1)
    return jnp.where(key_pos <= query_pos, scores, MASKED)


def attend_kernel(q_ref, k_ref, v_ref, out_ref, low_ref, stat_ref):
    row = pl.program_id(1)
    queries = q_ref[row, 0]

    def visit(block, carry, diagonal):
        top, total, acc = carry
        scores = dot(k_ref[block, 0], queries, 0, 0)
        if diagonal:
            scores = causal(scores)
        new_top = jnp.maximum(top, jnp.max(scores, axis=0, keepdims=True))
        scale = jnp.exp(top - new_top)
        weights = jnp.exp(scores - new_top)
        total = total * scale + jnp.sum(weights, axis=0, keepdims=True)
        acc = acc * scale + dot(v_ref[block, 0], weights.astype(jnp.bfloat16), 1, 0)
        return (new_top, total, acc)

    features, rows = queries.shape
    start = (
        jnp.full((1, rows), MASKED, jnp.float32),
        jnp.zeros((1, rows), jnp.float32),
        jnp.zeros((features, rows), jnp.float32),
    )
    carry = lax.fori_loop(0, row, lambda block, carry: visit(block, carry, False), start)
    top, total, acc = visit(row, carry, True)
    result = acc / total
    out_ref[0, 0] = result
    low_ref[0, 0] = result.astype(jnp.bfloat16)
    stat_ref[0, 0] = top + jnp.log(total)


def attend(project):
    blocks, triple, features, rows = project.shape
    heads = triple // 3
    whole = (blocks, 1, features, rows)
    part = pl.BlockSpec((1, 1, features, rows), lambda h, i: (i, h, 0, 0))
    return pl.pallas_call(
        attend_kernel,
        grid=(heads, blocks),
        in_specs=[
            pl.BlockSpec(whole, lambda h, i: (0, h, 0, 0)),
            pl.BlockSpec(whole, lambda h, i: (0, heads + h, 0, 0)),
            pl.BlockSpec(whole, lambda h, i: (0, 2 * heads + h, 0, 0)),
        ],
        out_specs=[
            part,
            part,
            pl.BlockSpec((1, 1, 1, rows), lambda h, i: (i, h, 0, 0)),
        ],
        out_shape=[
            jax.ShapeDtypeStruct((blocks, heads, features, rows), jnp.float32),
            jax.ShapeDtypeStruct((blocks, heads, features, rows), jnp.bfloat16),
            jax.ShapeDtypeStruct((blocks, heads, 1, rows), jnp.float32),
        ],
        compiler_params=pltpu.CompilerParams(vmem_limit_bytes=40 * MIB),
        cost_estimate=pl.CostEstimate(
            flops=2 * heads * features * rows * rows * blocks * (blocks + 1),
            bytes_accessed=12 * heads * features * rows * blocks,
            transcendentals=heads * rows * rows * blocks * (blocks + 1) // 2,
        ),
    )(project, project, project)


def attend_back_kernel(
    q_ref, k_ref, v_ref, grad_ref, out_ref, stat_ref, dq_ref, dk_ref, dv_ref, dk_acc, dv_acc
):
    row = pl.program_id(1)
    queries = q_ref[row, 0]
    grad = grad_ref[0, 0]
    stat = stat_ref[0, 0]
    delta = jnp.sum(grad.astype(jnp.float32) * out_ref[0, 0], axis=0, keepdims=True)

    def visit(block, acc, diagonal):
        keys = k_ref[block, 0]
        scores = dot(keys, queries, 0, 0)
        if diagonal:
            scores = causal(scores)
        probs = jnp.exp(scores - stat)
        grad_probs = dot(v_ref[block, 0], grad, 0, 0)
        grad_scores = (probs * (grad_probs - delta)).astype(jnp.bfloat16)
        key_part = dot(queries, grad_scores, 1, 1)
        value_part = dot(grad, probs.astype(jnp.bfloat16), 1, 1)
        if diagonal:
            dk_acc[block] = key_part
            dv_acc[block] = value_part
        else:
            dk_acc[block] += key_part
            dv_acc[block] += value_part
        return acc + dot(keys, grad_scores, 1, 0)

    acc = visit(row, jnp.zeros(queries.shape, jnp.float32), True)
    acc = lax.fori_loop(0, row, lambda block, acc: visit(block, acc, False), acc)
    dq_ref[0, 0] = acc.astype(jnp.bfloat16) * 0.125

    @pl.when(row == pl.num_programs(1) - 1)
    def _():
        dk_ref[:, 0] = dk_acc[...].astype(jnp.bfloat16)
        dv_ref[:, 0] = dv_acc[...].astype(jnp.bfloat16)


def attend_back(project, grad, outputs, stat):
    blocks, triple, features, rows = project.shape
    heads = triple // 3
    whole = (blocks, 1, features, rows)
    part = pl.BlockSpec((1, 1, features, rows), lambda h, i: (i, h, 0, 0))
    all_rows = pl.BlockSpec(whole, lambda h, i: (0, h, 0, 0))
    like = jax.ShapeDtypeStruct((blocks, heads, features, rows), jnp.bfloat16)
    return pl.pallas_call(
        attend_back_kernel,
        grid=(heads, blocks),
        in_specs=[
            all_rows,
            pl.BlockSpec(whole, lambda h, i: (0, heads + h, 0, 0)),
            pl.BlockSpec(whole, lambda h, i: (0, 2 * heads + h, 0, 0)),
            part,
            part,
            pl.BlockSpec((1, 1, 1, rows), lambda h, i: (i, h, 0, 0)),
        ],
        out_specs=[part, all_rows, all_rows],
        out_shape=[like, like, like],
        scratch_shapes=[
            pltpu.VMEM((blocks, features, rows), jnp.float32),
            pltpu.VMEM((blocks, features, rows), jnp.float32),
        ],
        compiler_params=pltpu.CompilerParams(vmem_limit_bytes=40 * MIB),
        cost_estimate=pl.CostEstimate(
            flops=5 * heads * features * rows * rows * blocks * (blocks + 1),
            bytes_accessed=20 * heads * features * rows * blocks,
            transcendentals=heads * rows * rows * blocks * (blocks + 1) // 2,
        ),
    )(project, project, project, grad, outputs, stat)


def exchange(value):
    return lax.all_to_all(value, "ctx", 0, 0, tiled=True)


def as_column(vector):
    return vector.astype(jnp.float32)[:, None]


def layer_forward(inputs, weights, vectors, heads):
    w_qkv, w_out, w_up, w_down = weights
    gain_one, shift_one, q_bias, v_bias, out_bias, gain_two, shift_two, up_bias, down_bias = vectors
    rows, width = inputs.shape
    ranks = lax.axis_size("ctx")
    normed, norm_one_back = jax.vjp(layer_norm, inputs, gain_one, shift_one)
    normed_low = normed.astype(jnp.bfloat16)
    project = dot(w_qkv, normed_low, 0, 1)
    queries = ((project[:width] + q_bias[:, None]) * 0.125).astype(jnp.bfloat16)
    keys = project[width : 2 * width].astype(jnp.bfloat16)
    values = (project[2 * width :] + v_bias[:, None]).astype(jnp.bfloat16)
    parts = [value.reshape(ranks, width // ranks, rows) for value in (queries, keys, values)]
    sent = jnp.concatenate(parts, axis=1)
    features = width // heads
    heads_all = exchange(sent).reshape(ranks, 3 * heads // ranks, features, rows)
    attended, attended_heads, stat = attend(heads_all)
    attended_low = exchange(attended_heads.reshape(ranks, width // ranks, rows)).reshape(width, rows)
    middle = inputs + matmul_left_t(attended_low, w_out) + out_bias
    normed_two, norm_two_back = jax.vjp(layer_norm, middle, gain_two, shift_two)
    normed_two_low = normed_two.astype(jnp.bfloat16)
    lifted = matmul(normed_two_low, w_up) + up_bias
    activated_low = smooth(lifted).astype(jnp.bfloat16)
    result = middle + matmul(activated_low, w_down) + down_bias
    record = (
        norm_one_back,
        normed_low,
        heads_all,
        attended,
        stat,
        attended_low,
        norm_two_back,
        normed_two_low,
        lifted,
        activated_low,
    )
    return (result, record)


def layer_backward(grad_result, weights, record):
    w_qkv, w_out, w_up, w_down = weights
    (
        norm_one_back,
        normed_low,
        heads_all,
        attended,
        stat,
        attended_low,
        norm_two_back,
        normed_two_low,
        lifted,
        activated_low,
    ) = record
    rows, width = grad_result.shape
    ranks = lax.axis_size("ctx")
    result_low = grad_result.astype(jnp.bfloat16)
    grad_down_bias = jnp.sum(grad_result, axis=0)
    grad_w_down = matmul_left_t(activated_low, result_low)
    grad_activated = matmul_right_t(result_low, w_down)
    _, smooth_back = jax.vjp(smooth, lifted)
    (grad_lifted,) = smooth_back(grad_activated)
    grad_up_bias = jnp.sum(grad_lifted, axis=0)
    lifted_low = grad_lifted.astype(jnp.bfloat16)
    grad_w_up = matmul_left_t(normed_two_low, lifted_low)
    grad_normed_two = matmul_right_t(lifted_low, w_up)
    middle_part, grad_gain_two, grad_shift_two = norm_two_back(grad_normed_two)
    grad_middle = grad_result + middle_part
    middle_low = grad_middle.astype(jnp.bfloat16)
    grad_out_bias = jnp.sum(grad_middle, axis=0)
    grad_w_out = matmul(attended_low, middle_low)
    grad_attended = dot(w_out, middle_low, 1, 1).astype(jnp.bfloat16)
    sent = grad_attended.reshape(ranks, width // ranks, rows)
    grad_heads = exchange(sent).reshape(attended.shape)
    pieces = attend_back(heads_all, grad_heads, attended, stat)
    home = jnp.concatenate([piece.reshape(ranks, 1, width // ranks, rows) for piece in pieces], 1)
    home = exchange(home)
    grad_project = jnp.swapaxes(home, 0, 1).reshape(3 * width, rows)
    grad_q_bias = jnp.sum(grad_project[:width].astype(jnp.float32), axis=1)
    grad_v_bias = jnp.sum(grad_project[2 * width :].astype(jnp.float32), axis=1)
    grad_w_qkv = dot(normed_low, grad_project, 0, 1)
    grad_normed = dot(grad_project, w_qkv, 0, 1)
    input_part, grad_gain_one, grad_shift_one = norm_one_back(grad_normed)
    grad_input = grad_middle + input_part
    grad_weights = (grad_w_qkv, grad_w_out, grad_w_up, grad_w_down)
    grad_vectors = (
        grad_gain_one,
        grad_shift_one,
        grad_q_bias,
        grad_v_bias,
        grad_out_bias,
        grad_gain_two,
        grad_shift_two,
        grad_up_bias,
        grad_down_bias,
    )
    return (grad_input, grad_weights, grad_vectors)


def gather_vectors(vectors):
    layers = vectors[0].shape[0]
    ranks = lax.axis_size("fsdp")
    packed = jnp.concatenate(vectors, axis=1)
    full = lax.all_gather(packed, "fsdp", axis=0)
    results = []
    start = 0
    for vector in vectors:
        piece = full[:, :, start : start + vector.shape[1]]
        start += vector.shape[1]
        results.append(jnp.swapaxes(piece, 0, 1).reshape(layers, -1).astype(jnp.float32))
    return [tuple(result[layer] for result in results) for layer in range(layers)]


def reduce_vectors(layer_grads):
    layers = len(layer_grads)
    ranks = lax.axis_size("fsdp")
    columns = [jnp.stack(each).reshape(layers, ranks, -1) for each in zip(*layer_grads)]
    packed = jnp.concatenate(columns, axis=2)
    packed = jnp.swapaxes(packed, 0, 1)
    total = lax.psum(packed, ("ctx", "fsdp"))
    own = lax.dynamic_index_in_dim(total, lax.axis_index("fsdp"), 0, keepdims=False)
    results = []
    start = 0
    for column in columns:
        results.append(own[:, start : start + column.shape[2]])
        start += column.shape[2]
    return results


def gather_weight(shard):
    return lax.all_gather(shard, "fsdp", axis=0, tiled=True)


def reduce_weight(grad):
    part = lax.psum_scatter(
        grad.astype(jnp.bfloat16), "fsdp", scatter_dimension=0, tiled=True
    )
    return lax.psum(part, "ctx").astype(jnp.float32)


def per_device(
    tokens,
    cotangent,
    ln1_gain,
    ln1_bias,
    w_qkv,
    q_bias,
    v_bias,
    w_out,
    out_bias,
    ln2_gain,
    ln2_bias,
    w_up,
    up_bias,
    w_down,
    down_bias,
):
    layers = w_qkv.shape[0]
    vectors = gather_vectors(
        (ln1_gain, ln1_bias, q_bias, v_bias, out_bias, ln2_gain, ln2_bias, up_bias, down_bias)
    )
    weights = [
        tuple(gather_weight(shard[layer]) for shard in (w_qkv, w_out, w_up, w_down))
        for layer in range(layers)
    ]
    hidden = tokens[0].astype(jnp.float32)
    records = []
    for layer in range(layers):
        hidden, record = layer_forward(hidden, weights[layer], vectors[layer], HEADS)
        records.append(record)
    outputs = hidden.astype(jnp.bfloat16)[None]
    grad_hidden = cotangent[0].astype(jnp.float32)
    weight_grads = [None] * layers
    vector_grads = [None] * layers
    for layer in reversed(range(layers)):
        grad_hidden, grads, vector_grads[layer] = layer_backward(
            grad_hidden, weights[layer], records[layer]
        )
        weight_grads[layer] = tuple(reduce_weight(grad) for grad in grads)
    g_qkv, g_out, g_up, g_down = (jnp.stack(each) for each in zip(*weight_grads))
    v1, v2, v3, v4, v5, v6, v7, v8, v9 = reduce_vectors(vector_grads)
    return (
        outputs,
        grad_hidden[None],
        v1,
        v2,
        g_qkv,
        v3,
        v4,
        g_out,
        v5,
        v6,
        v7,
        g_up,
        v8,
        g_down,
        v9,
    )


def solution(mesh):
    block = P("fsdp", "ctx", None)
    vector = P(None, "fsdp")
    matrix = P(None, "fsdp", None)
    params = (
        vector,
        vector,
        matrix,
        vector,
        vector,
        matrix,
        vector,
        vector,
        vector,
        matrix,
        vector,
        matrix,
        vector,
    )
    return jax.shard_map(
        per_device,
        mesh=mesh,
        in_specs=(block, block) + params,
        out_specs=(block, block) + params,
        check_vma=False,
    )
```

```python
import functools

import jax
import jax.numpy as jnp
from jax import lax
from jax.experimental import pallas as pl
from jax.experimental.pallas import tpu as pltpu
from jax.sharding import PartitionSpec as P

HEADS = 12


EPS = 1e-05
MASKED = -1e30
MIB = 1024 * 1024


def layer_norm(values, gain, shift):
    center = values - jnp.mean(values, axis=-1, keepdims=True)
    spread = jnp.mean(center * center, axis=-1, keepdims=True)
    return center * lax.rsqrt(spread + EPS) * gain + shift


def smooth(values):
    return jax.nn.gelu(values, approximate=False)


def dot(left, right, left_dim, right_dim):
    return lax.dot_general(
        left, right, (((left_dim,), (right_dim,)), ((), ())), preferred_element_type=jnp.float32
    )


def matmul(left, right):
    return dot(left, right, 1, 0)


def matmul_left_t(left, right):
    return dot(left, right, 0, 0)


def matmul_right_t(left, right):
    return dot(left, right, 1, 1)


def causal(scores):
    key_pos = lax.broadcasted_iota(jnp.int32, scores.shape, 0)
    query_pos = lax.broadcasted_iota(jnp.int32, scores.shape, 1)
    return jnp.where(key_pos <= query_pos, scores, MASKED)


def attend_kernel(q_ref, k_ref, v_ref, out_ref, low_ref, stat_ref):
    row = pl.program_id(1)
    queries = q_ref[row, 0]

    def visit(block, carry, diagonal):
        top, total, acc = carry
        scores = dot(k_ref[block, 0], queries, 0, 0)
        if diagonal:
            scores = causal(scores)
        new_top = jnp.maximum(top, jnp.max(scores, axis=0, keepdims=True))
        scale = jnp.exp(top - new_top)
        weights = jnp.exp(scores - new_top)
        total = total * scale + jnp.sum(weights, axis=0, keepdims=True)
        acc = acc * scale + dot(v_ref[block, 0], weights.astype(jnp.bfloat16), 1, 0)
        return (new_top, total, acc)

    features, rows = queries.shape
    start = (
        jnp.full((1, rows), MASKED, jnp.float32),
        jnp.zeros((1, rows), jnp.float32),
        jnp.zeros((features, rows), jnp.float32),
    )
    carry = lax.fori_loop(0, row, lambda block, carry: visit(block, carry, False), start)
    top, total, acc = visit(row, carry, True)
    result = acc / total
    out_ref[0, 0] = result
    low_ref[0, 0] = result.astype(jnp.bfloat16)
    stat_ref[0, 0] = top + jnp.log(total)


def attend(project):
    blocks, triple, features, rows = project.shape
    heads = triple // 3
    whole = (blocks, 1, features, rows)
    part = pl.BlockSpec((1, 1, features, rows), lambda h, i: (i, h, 0, 0))
    return pl.pallas_call(
        attend_kernel,
        grid=(heads, blocks),
        in_specs=[
            pl.BlockSpec(whole, lambda h, i: (0, h, 0, 0)),
            pl.BlockSpec(whole, lambda h, i: (0, heads + h, 0, 0)),
            pl.BlockSpec(whole, lambda h, i: (0, 2 * heads + h, 0, 0)),
        ],
        out_specs=[
            part,
            part,
            pl.BlockSpec((1, 1, 1, rows), lambda h, i: (i, h, 0, 0)),
        ],
        out_shape=[
            jax.ShapeDtypeStruct((blocks, heads, features, rows), jnp.float32),
            jax.ShapeDtypeStruct((blocks, heads, features, rows), jnp.bfloat16),
            jax.ShapeDtypeStruct((blocks, heads, 1, rows), jnp.float32),
        ],
        compiler_params=pltpu.CompilerParams(vmem_limit_bytes=40 * MIB),
        cost_estimate=pl.CostEstimate(
            flops=2 * heads * features * rows * rows * blocks * (blocks + 1),
            bytes_accessed=12 * heads * features * rows * blocks,
            transcendentals=heads * rows * rows * blocks * (blocks + 1) // 2,
        ),
    )(project, project, project)


def attend_back_kernel(
    q_ref, k_ref, v_ref, grad_ref, out_ref, stat_ref, dq_ref, dk_ref, dv_ref, dk_acc, dv_acc
):
    row = pl.program_id(1)
    queries = q_ref[row, 0]
    grad = grad_ref[0, 0]
    stat = stat_ref[0, 0]
    delta = jnp.sum(grad.astype(jnp.float32) * out_ref[0, 0], axis=0, keepdims=True)

    def visit(block, acc, diagonal):
        keys = k_ref[block, 0]
        scores = dot(keys, queries, 0, 0)
        if diagonal:
            scores = causal(scores)
        probs = jnp.exp(scores - stat)
        grad_probs = dot(v_ref[block, 0], grad, 0, 0)
        grad_scores = (probs * (grad_probs - delta)).astype(jnp.bfloat16)
        key_part = dot(queries, grad_scores, 1, 1)
        value_part = dot(grad, probs.astype(jnp.bfloat16), 1, 1)
        if diagonal:
            dk_acc[block] = key_part
            dv_acc[block] = value_part
        else:
            dk_acc[block] += key_part
            dv_acc[block] += value_part
        return acc + dot(keys, grad_scores, 1, 0)

    acc = visit(row, jnp.zeros(queries.shape, jnp.float32), True)
    acc = lax.fori_loop(0, row, lambda block, acc: visit(block, acc, False), acc)
    dq_ref[0, 0] = acc.astype(jnp.bfloat16) * 0.125

    @pl.when(row == pl.num_programs(1) - 1)
    def _():
        dk_ref[:, 0] = dk_acc[...].astype(jnp.bfloat16)
        dv_ref[:, 0] = dv_acc[...].astype(jnp.bfloat16)


def attend_back(project, grad, outputs, stat):
    blocks, triple, features, rows = project.shape
    heads = triple // 3
    whole = (blocks, 1, features, rows)
    part = pl.BlockSpec((1, 1, features, rows), lambda h, i: (i, h, 0, 0))
    all_rows = pl.BlockSpec(whole, lambda h, i: (0, h, 0, 0))
    like = jax.ShapeDtypeStruct((blocks, heads, features, rows), jnp.bfloat16)
    return pl.pallas_call(
        attend_back_kernel,
        grid=(heads, blocks),
        in_specs=[
            all_rows,
            pl.BlockSpec(whole, lambda h, i: (0, heads + h, 0, 0)),
            pl.BlockSpec(whole, lambda h, i: (0, 2 * heads + h, 0, 0)),
            part,
            part,
            pl.BlockSpec((1, 1, 1, rows), lambda h, i: (i, h, 0, 0)),
        ],
        out_specs=[part, all_rows, all_rows],
        out_shape=[like, like, like],
        scratch_shapes=[
            pltpu.VMEM((blocks, features, rows), jnp.float32),
            pltpu.VMEM((blocks, features, rows), jnp.float32),
        ],
        compiler_params=pltpu.CompilerParams(vmem_limit_bytes=40 * MIB),
        cost_estimate=pl.CostEstimate(
            flops=5 * heads * features * rows * rows * blocks * (blocks + 1),
            bytes_accessed=20 * heads * features * rows * blocks,
            transcendentals=heads * rows * rows * blocks * (blocks + 1) // 2,
        ),
    )(project, project, project, grad, outputs, stat)


def exchange(value):
    return lax.all_to_all(value, "ctx", 0, 0, tiled=True)


def layer_forward(inputs, weights, vectors, heads):
    w_qkv, w_out, w_up, w_down = weights
    gain_one, shift_one, q_bias, v_bias, out_bias, gain_two, shift_two, up_bias, down_bias = vectors
    rows, width = inputs.shape
    ranks = lax.axis_size("ctx")
    normed, norm_one_back = jax.vjp(layer_norm, inputs, gain_one, shift_one)
    normed_low = normed.astype(jnp.bfloat16)
    project = dot(w_qkv, normed_low, 0, 1)
    queries = ((project[:width] + q_bias[:, None]) * 0.125).astype(jnp.bfloat16)
    keys = project[width : 2 * width].astype(jnp.bfloat16)
    values = (project[2 * width :] + v_bias[:, None]).astype(jnp.bfloat16)
    parts = [value.reshape(ranks, width // ranks, rows) for value in (queries, keys, values)]
    sent = jnp.concatenate(parts, axis=1)
    features = width // heads
    heads_all = exchange(sent).reshape(ranks, 3 * heads // ranks, features, rows)
    attended, attended_heads, stat = attend(heads_all)
    attended_low = exchange(attended_heads.reshape(ranks, width // ranks, rows)).reshape(width, rows)
    middle = inputs + matmul_left_t(attended_low, w_out) + out_bias
    normed_two, norm_two_back = jax.vjp(layer_norm, middle, gain_two, shift_two)
    normed_two_low = normed_two.astype(jnp.bfloat16)
    lifted = matmul(normed_two_low, w_up) + up_bias
    activated_low = smooth(lifted).astype(jnp.bfloat16)
    result = middle + matmul(activated_low, w_down) + down_bias
    record = (
        norm_one_back,
        normed_low,
        heads_all,
        attended,
        stat,
        attended_low,
        norm_two_back,
        normed_two_low,
        lifted,
        activated_low,
    )
    return (result, record)


def layer_backward(grad_result, weights, record, pending):
    w_qkv, w_out, w_up, w_down = weights
    (
        norm_one_back,
        normed_low,
        heads_all,
        attended,
        stat,
        attended_low,
        norm_two_back,
        normed_two_low,
        lifted,
        activated_low,
    ) = record
    rows, width = grad_result.shape
    ranks = lax.axis_size("ctx")
    result_low = grad_result.astype(jnp.bfloat16)
    grad_down_bias = jnp.sum(grad_result, axis=0)
    grad_w_down = matmul_left_t(activated_low, result_low).astype(jnp.bfloat16)
    grad_activated = matmul_right_t(result_low, w_down)
    grad_activated, grad_w_down = lax.optimization_barrier((grad_activated, grad_w_down))
    down = scatter(grad_w_down)
    _, smooth_back = jax.vjp(smooth, lifted)
    (grad_lifted,) = smooth_back(grad_activated)
    grad_up_bias = jnp.sum(grad_lifted, axis=0)
    lifted_low = grad_lifted.astype(jnp.bfloat16)
    grad_w_up = matmul_left_t(normed_two_low, lifted_low).astype(jnp.bfloat16)
    grad_normed_two = matmul_right_t(lifted_low, w_up)
    grad_normed_two, grad_w_up = lax.optimization_barrier((grad_normed_two, grad_w_up))
    up = scatter(grad_w_up)
    middle_part, grad_gain_two, grad_shift_two = norm_two_back(grad_normed_two)
    grad_middle = grad_result + middle_part
    middle_low = grad_middle.astype(jnp.bfloat16)
    grad_out_bias = jnp.sum(grad_middle, axis=0)
    grad_w_out = matmul(attended_low, middle_low)
    grad_attended = dot(w_out, middle_low, 1, 1).astype(jnp.bfloat16)
    sent = grad_attended.reshape(ranks, width // ranks, rows)
    grad_heads = exchange(sent).reshape(attended.shape)
    if pending is not None:
        grad_heads, pending = lax.optimization_barrier((grad_heads, pending))
    pieces = attend_back(heads_all, grad_heads, attended, stat)
    home = jnp.concatenate([piece.reshape(ranks, 1, width // ranks, rows) for piece in pieces], 1)
    home, down = lax.optimization_barrier((exchange(home), down))
    grad_project = jnp.swapaxes(home, 0, 1).reshape(3 * width, rows)
    grad_q_bias = jnp.sum(grad_project[:width].astype(jnp.float32), axis=1)
    grad_v_bias = jnp.sum(grad_project[2 * width :].astype(jnp.float32), axis=1)
    grad_w_qkv = dot(normed_low, grad_project, 0, 1)
    grad_normed = dot(grad_project, w_qkv, 0, 1)
    input_part, grad_gain_one, grad_shift_one = norm_one_back(grad_normed)
    grad_input = grad_middle + input_part
    grad_weights = (grad_w_qkv, grad_w_out, up, down)
    grad_vectors = (
        grad_gain_one,
        grad_shift_one,
        grad_q_bias,
        grad_v_bias,
        grad_out_bias,
        grad_gain_two,
        grad_shift_two,
        grad_up_bias,
        grad_down_bias,
    )
    return (grad_input, grad_weights, grad_vectors, pending)


def gather_vectors(vectors):
    layers = vectors[0].shape[0]
    ranks = lax.axis_size("fsdp")
    packed = jnp.concatenate(vectors, axis=1)
    full = lax.all_gather(packed, "fsdp", axis=0)
    results = []
    start = 0
    for vector in vectors:
        piece = full[:, :, start : start + vector.shape[1]]
        start += vector.shape[1]
        results.append(jnp.swapaxes(piece, 0, 1).reshape(layers, -1).astype(jnp.float32))
    return [tuple(result[layer] for result in results) for layer in range(layers)]


def reduce_vectors(layer_grads):
    layers = len(layer_grads)
    ranks = lax.axis_size("fsdp")
    columns = [jnp.stack(each).reshape(layers, ranks, -1) for each in zip(*layer_grads)]
    packed = jnp.swapaxes(jnp.concatenate(columns, axis=2), 0, 1).reshape(ranks, -1)
    own = jnp.sum(lax.all_to_all(packed, "fsdp", 0, 0, tiled=True), axis=0)
    copies = jnp.broadcast_to(own[None], (lax.axis_size("ctx"),) + own.shape)
    own = jnp.sum(exchange(copies), axis=0).reshape(layers, -1)
    results = []
    start = 0
    for column in columns:
        results.append(own[:, start : start + column.shape[2]])
        start += column.shape[2]
    return results


def gather_weight(shard):
    return lax.all_gather(shard, "fsdp", axis=0, tiled=True)


def scatter(grad):
    return lax.psum_scatter(grad, "fsdp", scatter_dimension=0, tiled=True)


def add_blocks(value):
    return jnp.sum(exchange(value).astype(jnp.float32), axis=0).astype(jnp.bfloat16)


def block_share(grad):
    shards, ranks = lax.axis_size("fsdp"), lax.axis_size("ctx")
    rows, columns = grad.shape
    split = grad.reshape(shards, ranks, rows // (shards * ranks), columns)
    share = add_blocks(jnp.swapaxes(split, 0, 1))
    return share.reshape(rows // ranks, columns)


def reduce_weights(grads):
    g_qkv, g_out, up, down = grads
    g_qkv, g_out = g_qkv.astype(jnp.bfloat16), g_out.astype(jnp.bfloat16)
    ranks = lax.axis_size("ctx")
    width = g_qkv.shape[0]
    first = jnp.concatenate(
        [down.reshape(ranks, -1, width), up.reshape(ranks, -1, width)], axis=1
    )
    late = block_share(jnp.concatenate([g_qkv, g_out], axis=1))
    last = scatter(late)
    first, _ = lax.optimization_barrier((first, late))
    summed = add_blocks(first)
    share = jnp.concatenate([summed, last.reshape(-1, width)], axis=0)
    full = exchange(jnp.broadcast_to(share[None], (ranks,) + share.shape)).astype(jnp.float32)
    down_rows = down.size // (ranks * width)
    up_rows = up.size // (ranks * width)
    down = full[:, :down_rows].reshape(down.shape)
    up = full[:, down_rows : down_rows + up_rows].reshape(up.shape)
    rest = full[:, down_rows + up_rows :].reshape(-1, g_qkv.shape[1] + g_out.shape[1])
    return (rest[:, : g_qkv.shape[1]], rest[:, g_qkv.shape[1] :], up, down)


def per_device(
    tokens,
    cotangent,
    ln1_gain,
    ln1_bias,
    w_qkv,
    q_bias,
    v_bias,
    w_out,
    out_bias,
    ln2_gain,
    ln2_bias,
    w_up,
    up_bias,
    w_down,
    down_bias,
):
    layers = w_qkv.shape[0]
    vectors = gather_vectors(
        (ln1_gain, ln1_bias, q_bias, v_bias, out_bias, ln2_gain, ln2_bias, up_bias, down_bias)
    )
    weights = [
        tuple(gather_weight(shard[layer]) for shard in (w_qkv, w_out, w_up, w_down))
        for layer in range(layers)
    ]
    hidden = tokens[0].astype(jnp.float32)
    records = []
    for layer in range(layers):
        hidden, record = layer_forward(hidden, weights[layer], vectors[layer], HEADS)
        records.append(record)
    outputs = hidden.astype(jnp.bfloat16)[None]
    grad_hidden = cotangent[0].astype(jnp.float32)
    weight_grads = [None] * layers
    vector_grads = [None] * layers
    pending = None
    for layer in reversed(range(layers)):
        grad_hidden, grads, vector_grads[layer], tied = layer_backward(
            grad_hidden, weights[layer], records[layer], pending
        )
        if tied is not None:
            q_part, o_part, _, d_part = weight_grads[layer + 1]
            weight_grads[layer + 1] = (q_part, o_part, tied, d_part)
        weight_grads[layer] = grads
        pending = grads[2]
    weight_grads = [reduce_weights(grads) for grads in weight_grads]
    g_qkv, g_out, g_up, g_down = (jnp.stack(each) for each in zip(*weight_grads))
    v1, v2, v3, v4, v5, v6, v7, v8, v9 = reduce_vectors(vector_grads)
    return (
        outputs,
        grad_hidden[None],
        v1,
        v2,
        g_qkv,
        v3,
        v4,
        g_out,
        v5,
        v6,
        v7,
        g_up,
        v8,
        g_down,
        v9,
    )


def solution(mesh):
    block = P("fsdp", "ctx", None)
    vector = P(None, "fsdp")
    matrix = P(None, "fsdp", None)
    params = (
        vector,
        vector,
        matrix,
        vector,
        vector,
        matrix,
        vector,
        vector,
        vector,
        matrix,
        vector,
        matrix,
        vector,
    )
    return jax.shard_map(
        per_device,
        mesh=mesh,
        in_specs=(block, block) + params,
        out_specs=(block, block) + params,
        check_vma=False,
    )
```
